256 devices in a mesh: segment: 8 (over z_lo, y), dp: 32 (over z_hi, x, core).
Axes of the slice: x: 4, y: 4, z: 8 (z_hi: 4, z_lo: 2; z = z_hi * 2 + z_lo), core: 2. Of those that a mesh axis runs over, the one named last changes fastest.
Arguments:
- handoff: float32 [8, 128, 8, 8, 512], P('segment', 'dp'), parts along dimension 1, may hold values from -6 to 6
- fresh: float32 [4, 128, 8, 8, 512], P(None, 'dp'), parts along dimension 1, may hold values from -6 to 6
- skip_queue: float32 [8, 7, 128, 8, 8, 512], P('segment', None, 'dp'), parts along dimension 2, may hold values from -6 to 6
- conv_weight: bfloat16 [8, 2, 4608, 512], P('segment'), may hold values from -0.09375 to 0.09375
- norm_gain: float32 [8, 2, 512], P('segment'), may hold values from 0.5 to 1.5
- norm_shift: float32 [8, 2, 512], P('segment'), may hold values from -3 to 3
Outputs:
- activations: float32 [8, 5, 128, 8, 8, 512], P('segment', None, 'dp'), parts along dimension 2
- queue_out: float32 [8, 7, 128, 8, 8, 512], P('segment', None, 'dp'), parts along dimension 2
The draws below stay inside these ranges and needn't reach their ends.
There are 32 independent parts, one for each index of `dp`. The reference program is written for one: setup_inputs(seed, part) draws one part's arguments, and reference() takes and returns one part's arrays. A program takes and returns all parts, laid end to end along the dimension named above; an argument that names none is the same for every part. Nothing has to cross between parts.
All inputs are finite; a program needn't handle non-finite values.
Results may differ from the reference program's by a relative error of at most 0.004.
Values sent between devices are 32-bit elements; how exact they have to be, the bound alone decides.
A program may use at most 128 MiB of HBM per device.

```python
import jax
import jax.numpy as jnp
from jax import lax

C = 512
GROUP = 16
H = 8
W = 8
MICRO = 4
TICKS = 5
SECTIONS = 8
QUEUE = 7
N_SEGMENT = 8


def steps_of(stream_key, dims, pieces, smallest, largest):
    def one(dim, parts):
        steps = jax.random.uniform(jax.random.fold_in(jax.random.fold_in(stream_key, 6), dim), (parts,), jnp.float32, smallest / len(pieces), largest / len(pieces))
        return jnp.repeat(jnp.exp(steps), dims[dim] // parts).reshape((-1,) + (1,) * (len(dims) - dim - 1))

    level = one(*pieces[0])
    for cut in pieces[1:]:
        level = level * one(*cut)
    return level


def gaussian(rng, extent, width, bound, cuts=(), dtype=jnp.bfloat16):
    values = jax.random.normal(rng, extent, jnp.float32) * width
    if len(cuts) > 0:
        values = steps_of(rng, extent, cuts, -0.22, 0.18) * values
    return jnp.clip(values, min=-bound, max=bound).astype(dtype)


def setup_inputs(seed: int = 0, part: int = 0) -> dict:
    keys = jax.random.split(jax.random.key(seed), 7)
    own_keys = jax.random.split(jax.random.fold_in(keys[6], part), 7)
    return {
        "handoff": gaussian(own_keys[0], (SECTIONS, MICRO, H, W, C), 1.0, 6.0, ((0, 8),), jnp.float32),
        "fresh": gaussian(own_keys[1], (TICKS - 1, MICRO, H, W, C), 1.0, 6.0, (), jnp.float32),
        "skip_queue": gaussian(own_keys[2], (SECTIONS, QUEUE, MICRO, H, W, C), 1.0, 6.0, ((0, 8),), jnp.float32),
        "conv_weight": gaussian(keys[3], (SECTIONS, 2, 9 * C, C), (9 * C) ** -0.5, 0.09375, ((0, 8),)),
        "norm_gain": jnp.clip(1.0 + 0.1 * jax.random.normal(keys[4], (SECTIONS, 2, C), jnp.float32), 0.5, 1.5),
        "norm_shift": gaussian(keys[5], (SECTIONS, 2, C), 0.5, 3.0, ((0, 8),), jnp.float32),
    }


norm_eps = 1e-05

def group_silu(field, gain_row, shift_row):
    images, height_cells, width_cells, channels = field.shape
    grouped = field.reshape(images, height_cells * width_cells, channels // GROUP, GROUP)
    average = lax.optimization_barrier(jnp.mean(grouped, axis=(1, 3), keepdims=True))
    spread = lax.optimization_barrier(jnp.mean(jnp.square(grouped - average), axis=(1, 3), keepdims=True))
    normed = ((grouped - average) * lax.rsqrt(spread + norm_eps)).reshape(field.shape)
    scaled = normed * gain_row + shift_row
    return jax.nn.silu(scaled).astype(jnp.bfloat16)

def convolve(activated, kernel):
    images, height_cells, width_cells, channels = activated.shape
    padded = jnp.pad(activated, ((0, 0), (1, 1), (1, 1), (0, 0)))
    patches = jnp.concatenate([padded[:, row_off:row_off + height_cells, col_off:col_off + width_cells, :] for row_off in range(3) for col_off in range(3)], axis=3)
    product = jnp.dot(patches.reshape(images * height_cells * width_cells, 9 * channels), kernel, preferred_element_type=jnp.float32)
    return product.reshape(images, height_cells, width_cells, kernel.shape[1])

def section(entering, skip_map, kernels, gain_rows, shift_rows, is_encoder):
    first_conv = convolve(group_silu(entering, gain_rows[0], shift_rows[0]), kernels[0])
    feed_map = jnp.where(is_encoder, first_conv, skip_map)
    second = convolve(group_silu(feed_map, gain_rows[1], shift_rows[1]), kernels[1])
    return entering + second + jnp.where(is_encoder, jnp.float32(0.0), first_conv)

def reference(handoff, fresh, skip_queue, conv_weight, norm_gain, norm_shift):
    section_ids = jnp.arange(N_SEGMENT)
    is_encoder = section_ids < N_SEGMENT // 2
    queue_depth = 2 * section_ids - N_SEGMENT + 1
    slot_ids = jnp.arange(QUEUE)
    insert = (slot_ids[None, :] == queue_depth[:, None] - 1) & jnp.logical_not(is_encoder)[:, None]
    filled = (slot_ids[None, :] < queue_depth[:, None]) & jnp.logical_not(is_encoder)[:, None]
    inputs_now = handoff
    pending = skip_queue
    history = []
    for tick_index in range(TICKS):
        result = lax.map(lambda packed: section(*packed), (inputs_now, pending[:, 0], conv_weight, norm_gain, norm_shift, is_encoder))
        history.append(result)
        received = result[::-1]
        shifted = jnp.concatenate([pending[:, 1:], jnp.zeros_like(pending[:, :1])], axis=1)
        pending = jnp.where(insert[:, :, None, None, None, None], received[:, None], shifted)
        if tick_index + 1 < TICKS:
            inputs_now = jnp.concatenate([fresh[tick_index][None], result[:-1]], axis=0)
    activations = jnp.stack(history, axis=1)
    queue_out = jnp.where(filled[:, :, None, None, None, None], pending, jnp.float32(0.0))
    return (activations, queue_out)
```

```python
import functools

import jax
import jax.numpy as jnp
from jax import lax
from jax.experimental import pallas as pl
from jax.experimental.pallas import tpu as pltpu
from jax.sharding import PartitionSpec as P

MESH = pl.DeviceIdType.MESH
GROUP = 16
EPS = 1e-05
SIDE = 8
CELLS = SIDE * SIDE
LAG = 2


def group_stats(x):
    cells, channels = x.shape
    mean = jnp.mean(x, axis=0, keepdims=True)
    spread = jnp.mean(jnp.square(x - mean), axis=0, keepdims=True)
    lane = lax.broadcasted_iota(jnp.int32, (1, channels), 1)
    for step in (1, 2, 4, 8):
        upper = (lane & step) != 0
        other_mean = jnp.where(upper, pltpu.roll(mean, step, 1), pltpu.roll(mean, channels - step, 1))
        other_spread = jnp.where(upper, pltpu.roll(spread, step, 1), pltpu.roll(spread, channels - step, 1))
        half = 0.5 * (mean - other_mean)
        mean = 0.5 * (mean + other_mean)
        spread = 0.5 * (spread + other_spread) + half * half
    return mean, spread


def fill_patches(x, gain, shift, patches):
    cells, channels = x.shape
    mean, spread = group_stats(x)
    u = (x - mean) * lax.rsqrt(spread + EPS) * gain + shift
    a = u / (1.0 + jnp.exp(-u))
    column = lax.broadcasted_iota(jnp.int32, (cells, channels), 0) % SIDE
    edge = jnp.zeros((SIDE, channels), jnp.float32)
    for c in range(3):
        if c == 0:
            moved = jnp.where(column == 0, 0.0, pltpu.roll(a, 1, 0))
        elif c == 2:
            moved = jnp.where(column == SIDE - 1, 0.0, pltpu.roll(a, cells - 1, 0))
        else:
            moved = a
        for r in range(3):
            if r == 0:
                rows = jnp.concatenate([edge, moved[:-SIDE]], axis=0)
            elif r == 2:
                rows = jnp.concatenate([moved[SIDE:], edge], axis=0)
            else:
                rows = moved
            k = 3 * r + c
            patches[:, k * channels : (k + 1) * channels] = rows.astype(jnp.bfloat16)


def window(
    images,
    ticks,
    handoff,
    fresh,
    skips,
    weights,
    gain,
    shift,
    act,
    queue,
    w,
    x_in,
    out_v,
    mirror,
    q,
    feed,
    patches,
    load_sem,
    hand_send,
    hand_recv,
    mir_send,
    mir_recv,
    rel_send,
    out_sem,
):
    s = lax.axis_index("segment")
    sections = 8
    steps = images * ticks
    handed = images * (ticks - 1)
    encoder = s < sections // 2

    load_x = pltpu.make_async_copy(handoff, x_in.at[pl.ds(0, images)], load_sem.at[0])
    load_w = [pltpu.make_async_copy(weights.at[k], w.at[k], load_sem.at[1 + k]) for k in range(2)]
    load_fresh = pltpu.make_async_copy(fresh, x_in.at[pl.ds(images, handed)], load_sem.at[3])
    load_q = pltpu.make_async_copy(skips.at[pl.ds(0, steps)], q, load_sem.at[4])
    keep_q = pltpu.make_async_copy(
        skips.at[pl.ds(steps, 2 * images)], queue.at[pl.ds(0, 2 * images)], load_sem.at[5]
    )
    load_x.start()
    load_w[0].start()
    load_w[1].start()
    pl.when(s == 0)(load_fresh.start)
    pl.when(s >= sections // 2)(load_q.start)
    pl.when(s == sections - 1)(keep_q.start)

    barrier = pltpu.get_barrier_semaphore()
    for k in range(1, sections):
        pl.semaphore_signal(barrier, 1, device_id={"segment": lax.rem(s + k, sections)}, device_id_type=MESH)
    pl.semaphore_wait(barrier, sections - 1)

    def hand(n):
        return pltpu.make_async_remote_copy(
            out_v.at[n],
            x_in.at[n + images],
            hand_send.at[n],
            hand_recv.at[n + images],
            device_id={"segment": jnp.minimum(s + 1, sections - 1)},
            device_id_type=MESH,
        )

    def hand_arrived(n):
        pltpu.make_async_remote_copy(
            out_v.at[n],
            x_in.at[n],
            hand_send.at[n],
            hand_recv.at[n],
            device_id={"segment": jnp.minimum(s + 1, sections - 1)},
            device_id_type=MESH,
        ).wait_recv()

    def to_mirror(source, n, sem, target):
        return pltpu.make_async_remote_copy(
            source, mirror.at[n], sem, mir_recv.at[n], device_id={"segment": target}, device_id_type=MESH
        )

    def to_queue(source, n, slot, sem, target):
        return pltpu.make_async_remote_copy(
            source, queue.at[slot], sem, mir_recv.at[n], device_id={"segment": target}, device_id_type=MESH
        )

    def relay(m):
        to_mirror(mirror.at[m], m, rel_send.at[m], jnp.int32(1)).wait_recv()

        @pl.when(m < 2 * images)
        def _():
            to_mirror(mirror.at[m], m, rel_send.at[m], jnp.int32(5)).start()

        @pl.when(m >= 2 * images)
        def _():
            to_queue(mirror.at[m], m, m - 2 * images, rel_send.at[m], jnp.int32(5)).start()

    load_x.wait()
    load_w[0].wait()

    def step(n, carry):
        @pl.when((s == 0) & (n == images))
        def _():
            load_fresh.wait()

        @pl.when((s > 0) & (n >= images))
        def _():
            hand_arrived(n)

        @pl.when((s == 2) & (n >= images))
        def _():
            to_queue(x_in.at[n], n - images, n - images, rel_send.at[n - images], jnp.int32(6)).start()

        @pl.when((s == 1) & (n >= LAG) & (n < handed + LAG))
        def _():
            relay(n - LAG)

        @pl.when(n == 0)
        def _():
            load_w[1].wait()

        @pl.when((s >= sections // 2) & (n == 0))
        def _():
            load_q.wait()

        fill_patches(x_in[n], gain[0:1], shift[0:1], patches.at[0])
        first = jnp.dot(patches[0], w[0], preferred_element_type=jnp.float32)

        @pl.when(encoder)
        def _():
            feed[...] = first
            out_v[n] = x_in[n]

        @pl.when(jnp.logical_not(encoder))
        def _():
            out_v[n] = x_in[n] + first

        @pl.when((s == 4) & (n >= images))
        def _():
            feed[...] = x_in[n]

        @pl.when((s == 5) & (n >= 3 * images))
        def _():
            to_mirror(mirror.at[n - 3 * images], n - 3 * images, rel_send.at[n - 3 * images], jnp.int32(4)).wait_recv()
            feed[...] = mirror[n - 3 * images]

        @pl.when(
            ((s == 4) & (n < images)) | ((s == 5) & (n < 3 * images)) | (s >= 6)
        )
        def _():
            feed[...] = q[n]

        fill_patches(feed[...], gain[1:2], shift[1:2], patches.at[1])
        second = jnp.dot(patches[1], w[1], preferred_element_type=jnp.float32)
        out_v[n] = out_v[n] + second

        @pl.when((s < sections - 1) & (n < handed))
        def _():
            hand(n).start()

        @pl.when(s == 0)
        def _():
            to_queue(out_v.at[n], n, n + 2 * images, mir_send.at[n], jnp.int32(7)).start()

        @pl.when((s == 1) & (n >= handed))
        def _():
            to_queue(out_v.at[n], n, n, mir_send.at[n], jnp.int32(6)).start()

        @pl.when((s == 2) & (n < handed))
        def _():
            to_mirror(out_v.at[n], n, mir_send.at[n], jnp.int32(1)).start()

        @pl.when((s == 2) & (n >= handed))
        def _():
            to_queue(out_v.at[n], n, n - 2 * images, mir_send.at[n], jnp.int32(5)).start()

        @pl.when((s == 3) & (n >= handed))
        def _():
            to_queue(out_v.at[n], n, n - handed, mir_send.at[n], jnp.int32(4)).start()

        pltpu.make_async_copy(out_v.at[n], act.at[n], out_sem.at[n]).start()
        return carry

    lax.fori_loop(0, steps, step, 0)

    def drain(n, carry):
        @pl.when((s < sections - 1) & (n < handed))
        def _():
            hand(n).wait_send()

        @pl.when((s == 0) | (s == 2) | (((s == 1) | (s == 3)) & (n >= handed)))
        def _():
            to_mirror(out_v.at[n], n, mir_send.at[n], jnp.int32(7)).wait_send()

        @pl.when(((s == 1) | (s == 2)) & (n < handed))
        def _():
            to_mirror(out_v.at[n], n, rel_send.at[n], jnp.int32(6)).wait_send()

        @pl.when(((s == 4) & (n >= handed)) | ((s == 5) & (n >= 2 * images)) | (s >= 6))
        def _():
            to_queue(out_v.at[n], n, n, rel_send.at[n], jnp.int32(6)).wait_recv()

        pltpu.make_async_copy(out_v.at[n], act.at[n], out_sem.at[n]).wait()
        return carry

    lax.fori_loop(0, steps, drain, 0)
    pl.when(s == sections - 1)(keep_q.wait)


def per_device(handoff, fresh, skip_queue, conv_weight, norm_gain, norm_shift):
    _, images, height, width, channels = handoff.shape
    ticks = fresh.shape[0] + 1
    depth = skip_queue.shape[1]
    steps = images * ticks
    cells = height * width
    s = lax.axis_index("segment")
    f32 = jnp.float32
    anywhere = pl.BlockSpec(memory_space=pl.ANY)
    hbm = pl.BlockSpec(memory_space=pltpu.HBM)
    vmem = pl.BlockSpec(memory_space=pltpu.VMEM)
    act, queue = pl.pallas_call(
        functools.partial(window, images, ticks),
        out_shape=(
            jax.ShapeDtypeStruct((steps, cells, channels), f32),
            jax.ShapeDtypeStruct((images * depth, cells, channels), f32),
        ),
        in_specs=[hbm, hbm, hbm, hbm, vmem, vmem],
        out_specs=(anywhere, anywhere),
        scratch_shapes=[
            pltpu.VMEM((2, 9 * channels, channels), jnp.bfloat16),
            pltpu.VMEM((steps, cells, channels), f32),
            pltpu.VMEM((steps, cells, channels), f32),
            pltpu.VMEM((steps, cells, channels), f32),
            pltpu.VMEM((steps, cells, channels), f32),
            pltpu.VMEM((cells, channels), f32),
            pltpu.VMEM((2, cells, 9 * channels), jnp.bfloat16),
            pltpu.SemaphoreType.DMA((6,)),
            pltpu.SemaphoreType.DMA((steps,)),
            pltpu.SemaphoreType.DMA((steps,)),
            pltpu.SemaphoreType.DMA((steps,)),
            pltpu.SemaphoreType.DMA((steps,)),
            pltpu.SemaphoreType.DMA((steps,)),
            pltpu.SemaphoreType.DMA((steps,)),
        ],
        compiler_params=pltpu.CompilerParams(
            collective_id=0, has_side_effects=True, vmem_limit_bytes=36 << 20
        ),
        cost_estimate=pl.CostEstimate(
            flops=4 * steps * cells * 9 * channels * channels, bytes_accessed=20 << 20, transcendentals=0
        ),
        name="window",
    )(
        pltpu.with_memory_space_constraint(handoff.reshape(images, cells, channels), pltpu.HBM),
        pltpu.with_memory_space_constraint(fresh.reshape(steps - images, cells, channels), pltpu.HBM),
        pltpu.with_memory_space_constraint(skip_queue.reshape(images * depth, cells, channels), pltpu.HBM),
        pltpu.with_memory_space_constraint(conv_weight[0], pltpu.HBM),
        pltpu.with_memory_space_constraint(norm_gain[0], pltpu.HBM),
        pltpu.with_memory_space_constraint(norm_shift[0], pltpu.HBM),
    )
    filled = jnp.arange(depth) < jnp.where(s >= 4, 2 * s - 7, 0)
    queue = queue.reshape(depth, images, height, width, channels)
    queue = jnp.where(filled[:, None, None, None, None], queue, jnp.float32(0.0))
    return act.reshape(1, ticks, images, height, width, channels), queue[None]


def solution(mesh):
    return jax.shard_map(
        per_device,
        mesh=mesh,
        in_specs=(
            P("segment", "dp", None, None, None),
            P(None, "dp", None, None, None),
            P("segment", None, "dp", None, None, None),
            P("segment", None, None, None),
            P("segment", None, None),
            P("segment", None, None),
        ),
        out_specs=(
            P("segment", None, "dp", None, None, None),
            P("segment", None, "dp", None, None, None),
        ),
        check_vma=False,
    )
```

```python
import functools

import jax
import jax.numpy as jnp
from jax import lax
from jax.experimental import pallas as pl
from jax.experimental.pallas import tpu as pltpu
from jax.sharding import PartitionSpec as P

MESH = pl.DeviceIdType.MESH
EPS = 1e-05
SIDE = 8
LANES = 128
PAIR = 2
SECTIONS = 8


def merge_four(mean, spread, step):
    lane = lax.broadcasted_iota(jnp.int32, mean.shape, 1)
    digit = (lane // step) % 4

    def around(v):
        others = []
        for k in range(1, 4):
            ahead = pltpu.roll(v, LANES - k * step, 1)
            behind = pltpu.roll(v, (4 - k) * step, 1)
            others.append(jnp.where(digit < 4 - k, ahead, behind))
        return [v] + others

    means = around(mean)
    spreads = around(spread)
    mean = 0.25 * ((means[0] + means[1]) + (means[2] + means[3]))
    between = [jnp.square(m - mean) for m in means]
    spread = 0.25 * (
        ((spreads[0] + between[0]) + (spreads[1] + between[1]))
        + ((spreads[2] + between[2]) + (spreads[3] + between[3]))
    )
    return mean, spread


def fill_patches(x, gain, shift, patches):
    images, cells, channels = x.shape
    column = lax.broadcasted_iota(jnp.int32, (cells, LANES), 0) % SIDE
    edge = jnp.zeros((SIDE, LANES), jnp.float32)
    for lo in range(0, channels, LANES):
        part = x[:, :, lo : lo + LANES]
        mean = jnp.mean(part, axis=1)
        spread = jnp.mean(jnp.square(part - mean[:, None]), axis=1)
        for step in (1, 4):
            mean, spread = merge_four(mean, spread, step)
        scale = lax.rsqrt(spread + EPS) * gain[:, lo : lo + LANES]
        for image in range(images):
            u = (part[image] - mean[image : image + 1]) * scale[image : image + 1] + shift[:, lo : lo + LANES]
            a = u / (1.0 + jnp.exp(-u))
            for c in range(3):
                if c == 0:
                    moved = jnp.where(column == 0, 0.0, pltpu.roll(a, 1, 0))
                elif c == 2:
                    moved = jnp.where(column == SIDE - 1, 0.0, pltpu.roll(a, cells - 1, 0))
                else:
                    moved = a
                for r in range(3):
                    if r == 0:
                        rows = jnp.concatenate([edge, moved[:-SIDE]], axis=0)
                    elif r == 2:
                        rows = jnp.concatenate([moved[SIDE:], edge], axis=0)
                    else:
                        rows = moved
                    at = (3 * r + c) * channels + lo
                    patches[image * cells : (image + 1) * cells, at : at + LANES] = rows.astype(jnp.bfloat16)


def window(
    images,
    ticks,
    handoff,
    fresh,
    skips,
    weights,
    gains,
    shifts,
    act,
    queue,
    w,
    gain,
    shift,
    bank,
    out_v,
    patches,
    load_sem,
    hand_send,
    hand_recv,
    mir_send,
    mir_recv,
    rel_send,
    out_sem,
):
    s = lax.axis_index("segment")
    steps = images * ticks
    handed = images * (ticks - 1)
    pairs = steps // PAIR
    half = SECTIONS // 2
    encoder = s < half
    cells, channels = bank.shape[1:]
    side = steps
    spare = 2 * steps

    load_x = pltpu.make_async_copy(handoff, bank.at[pl.ds(0, images)], load_sem.at[0])
    load_w = [pltpu.make_async_copy(weights.at[k], w.at[k], load_sem.at[1 + k]) for k in range(2)]
    load_fresh = pltpu.make_async_copy(fresh, bank.at[pl.ds(images, handed)], load_sem.at[3])
    keep_q = pltpu.make_async_copy(
        skips.at[pl.ds(steps, 2 * images)], queue.at[pl.ds(0, 2 * images)], load_sem.at[5]
    )
    load_gain = pltpu.make_async_copy(gains, gain, load_sem.at[6])
    load_shift = pltpu.make_async_copy(shifts, shift, load_sem.at[7])

    def load_q(count):
        return pltpu.make_async_copy(
            skips.at[pl.ds(0, count)], bank.at[pl.ds(side, count)], load_sem.at[4]
        )

    own_skips = ((s == half, images), (s == half + 1, 3 * images), (s >= half + 2, steps))
    load_gain.start()
    load_shift.start()
    load_x.start()
    for here, count in own_skips:
        pl.when(here)(load_q(count).start)

    @pl.when(encoder)
    def _():
        load_w[0].start()
        load_w[1].start()

    @pl.when(jnp.logical_not(encoder))
    def _():
        load_w[1].start()
        load_w[0].start()

    pl.when(s == 0)(load_fresh.start)
    pl.when(s == SECTIONS - 1)(keep_q.start)

    barrier = pltpu.get_barrier_semaphore()
    for k in range(1, SECTIONS):
        pl.semaphore_signal(barrier, 1, device_id={"segment": lax.rem(s + k, SECTIONS)}, device_id_type=MESH)

    def to_bank(source, slot, send, recv, target):
        return pltpu.make_async_remote_copy(
            source, bank.at[slot], send, recv, device_id={"segment": target}, device_id_type=MESH
        )

    def to_queue(source, slot, send, recv, target):
        return pltpu.make_async_remote_copy(
            source, queue.at[slot], send, recv, device_id={"segment": target}, device_id_type=MESH
        )

    def hand(n):
        return to_bank(
            out_v.at[n],
            n + images,
            hand_send.at[n],
            hand_recv.at[n + images],
            jnp.minimum(s + 1, SECTIONS - 1),
        )

    def arrived(recv):
        to_bank(out_v.at[0], spare, hand_send.at[0], recv, jnp.int32(0)).wait_recv()

    def to_five(source, n, send):
        @pl.when(n < 2 * images)
        def _():
            to_bank(source, side + 3 * images + n, send, mir_recv.at[n], jnp.int32(5)).start()

        @pl.when(n >= 2 * images)
        def _():
            to_queue(source, n - 2 * images, send, mir_recv.at[n], jnp.int32(5)).start()

    def wait_x(p):
        @pl.when((s == 0) & (p == images // PAIR))
        def _():
            load_fresh.wait()

        for k in range(PAIR):
            n = p * PAIR + k

            @pl.when((s > 0) & (n >= images))
            def _():
                arrived(hand_recv.at[n])

            @pl.when((s == 2) & (n >= images))
            def _():
                m = n - images
                to_queue(bank.at[n], m, rel_send.at[m], mir_recv.at[m], jnp.int32(6)).start()

    def convolve(slot, kind):
        g = jnp.where(kind == 0, gain[0:1], gain[1:2])
        b = jnp.where(kind == 0, shift[0:1], shift[1:2])
        fill_patches(bank[pl.ds(slot, PAIR)], g, b, patches)
        return jnp.dot(patches[...], w[kind], preferred_element_type=jnp.float32).reshape(PAIR, cells, channels)

    def step(p, start):
        early = encoder | ((s == half) & (p * PAIR >= images))
        if not start:
            pl.when(early)(lambda: wait_x(p))

        @pl.when((s == half + 1) & (p * PAIR >= 3 * images))
        def _():
            for k in range(PAIR):
                arrived(mir_recv.at[p * PAIR + k - 3 * images])

        if start:
            load_gain.wait()
            load_shift.wait()
            load_x.wait()
            for here, count in own_skips:
                pl.when(here)(load_q(count).wait)
            pl.when(encoder)(load_w[0].wait)
            pl.when(jnp.logical_not(encoder))(load_w[1].wait)
        n = p * PAIR
        kind = jnp.where(encoder, 0, 1)
        first = convolve(jnp.where(early, n, side + n), kind)
        bank[pl.ds(spare, PAIR)] = first
        if start:
            pl.when(encoder)(load_w[1].wait)
            pl.when(jnp.logical_not(encoder))(load_w[0].wait)
        else:
            pl.when(jnp.logical_not(early))(lambda: wait_x(p))
        second = convolve(jnp.where(encoder, spare, n), 1 - kind)
        total = bank[pl.ds(n, PAIR)] + second
        out_v[pl.ds(n, PAIR)] = jnp.where(encoder, total, total + bank[pl.ds(spare, PAIR)])
        if start:
            pl.semaphore_wait(barrier, SECTIONS - 1)
        for k in range(PAIR):
            send(p * PAIR + k)
        if not start:
            for k in range(PAIR):
                relay((p - 1) * PAIR + k)

    def send(n):
        @pl.when((s < SECTIONS - 1) & (n < handed))
        def _():
            hand(n).start()

        @pl.when(s == 0)
        def _():
            to_queue(out_v.at[n], n + 2 * images, mir_send.at[n], mir_recv.at[n], jnp.int32(7)).start()

        @pl.when((s == 1) & (n >= handed))
        def _():
            to_queue(out_v.at[n], n, mir_send.at[n], mir_recv.at[n], jnp.int32(6)).start()

        @pl.when((s == 2) & (n >= PAIR) & (n < handed))
        def _():
            to_bank(out_v.at[n], side + n, mir_send.at[n], mir_recv.at[n], jnp.int32(1)).start()

        @pl.when((s == 2) & ((n < PAIR) | (n >= handed)))
        def _():
            to_five(out_v.at[n], n, mir_send.at[n])

        @pl.when((s == 3) & (n >= handed))
        def _():
            to_queue(out_v.at[n], n - handed, mir_send.at[n], mir_recv.at[n], jnp.int32(4)).start()

        pltpu.make_async_copy(out_v.at[n], act.at[n], out_sem.at[n]).start()

    def relay(m):
        @pl.when((s == 1) & (m >= PAIR) & (m < handed))
        def _():
            arrived(mir_recv.at[m])
            to_five(bank.at[side + m], m, rel_send.at[m])

    step(jnp.int32(0), True)
    lax.fori_loop(1, pairs, lambda p, carry: (step(p, False), carry)[1], 0)

    def drain(n, carry):
        @pl.when((s < SECTIONS - 1) & (n < handed))
        def _():
            hand(n).wait_send()

        @pl.when((s == 0) | (s == 2) | (((s == 1) | (s == 3)) & (n >= handed)))
        def _():
            to_bank(out_v.at[n], spare, mir_send.at[n], mir_recv.at[n], jnp.int32(7)).wait_send()

        @pl.when((((s == 1) & (n >= PAIR)) | (s == 2)) & (n < handed))
        def _():
            to_bank(out_v.at[n], spare, rel_send.at[n], mir_recv.at[n], jnp.int32(6)).wait_send()

        @pl.when(((s == 4) & (n >= handed)) | ((s == 5) & (n >= 2 * images)) | (s >= 6))
        def _():
            arrived(mir_recv.at[n])

        pltpu.make_async_copy(out_v.at[n], act.at[n], out_sem.at[n]).wait()
        return carry

    lax.fori_loop(0, steps, drain, 0)
    pl.when(s == SECTIONS - 1)(keep_q.wait)


def place(act, queue, act_out, queue_out, zeros, sem):
    s = lax.axis_index("segment")
    depth = jnp.where(s < SECTIONS // 2, 0, 2 * s - SECTIONS + 1)
    images = zeros.shape[0]
    slots = queue.shape[0] // images
    ticks = act.shape[0] // images
    for t in range(ticks):
        rows = pl.ds(t * images, images)
        pltpu.make_async_copy(act.at[rows], act_out.at[rows], sem.at[t]).start()
    for k in range(slots):
        rows = pl.ds(k * images, images)
        pl.when(k < depth)(pltpu.make_async_copy(queue.at[rows], queue_out.at[rows], sem.at[ticks + k]).start)
    zeros[...] = jnp.zeros_like(zeros)
    for k in range(slots):
        rows = pl.ds(k * images, images)
        pl.when(k >= depth)(pltpu.make_async_copy(zeros, queue_out.at[rows], sem.at[ticks + k]).start)
    for t in range(ticks):
        rows = pl.ds(t * images, images)
        pltpu.make_async_copy(act.at[rows], act_out.at[rows], sem.at[t]).wait()
    for k in range(slots):
        rows = pl.ds(k * images, images)
        pltpu.make_async_copy(zeros, queue_out.at[rows], sem.at[ticks + k]).wait()


def per_device(handoff, fresh, skip_queue, conv_weight, norm_gain, norm_shift):
    _, images, height, width, channels = handoff.shape
    ticks = fresh.shape[0] + 1
    depth = skip_queue.shape[1]
    steps = images * ticks
    cells = height * width
    f32 = jnp.float32
    anywhere = pl.BlockSpec(memory_space=pl.ANY)
    shapes = (
        jax.ShapeDtypeStruct((steps, cells, channels), f32),
        jax.ShapeDtypeStruct((images * depth, cells, channels), f32),
    )
    operands = (
        handoff.reshape(images, cells, channels),
        fresh.reshape(steps - images, cells, channels),
        skip_queue.reshape(images * depth, cells, channels),
        conv_weight[0],
        norm_gain[0],
        norm_shift[0],
    )
    made = pl.pallas_call(
        functools.partial(window, images, ticks),
        out_shape=shapes,
        in_specs=[anywhere] * 6,
        out_specs=(anywhere, anywhere),
        scratch_shapes=[
            pltpu.VMEM((2, 9 * channels, channels), jnp.bfloat16),
            pltpu.VMEM((2, channels), f32),
            pltpu.VMEM((2, channels), f32),
            pltpu.VMEM((2 * steps + PAIR, cells, channels), f32),
            pltpu.VMEM((steps, cells, channels), f32),
            pltpu.VMEM((PAIR * cells, 9 * channels), jnp.bfloat16),
            pltpu.SemaphoreType.DMA((8,)),
            pltpu.SemaphoreType.DMA((steps,)),
            pltpu.SemaphoreType.DMA((steps,)),
            pltpu.SemaphoreType.DMA((steps,)),
            pltpu.SemaphoreType.DMA((steps,)),
            pltpu.SemaphoreType.DMA((steps,)),
            pltpu.SemaphoreType.DMA((steps,)),
        ],
        compiler_params=pltpu.CompilerParams(
            collective_id=0, has_side_effects=True, vmem_limit_bytes=36 << 20
        ),
        cost_estimate=pl.CostEstimate(
            flops=4 * steps * cells * 9 * channels * channels, bytes_accessed=20 << 20, transcendentals=0
        ),
        name="window",
    )(*[pltpu.with_memory_space_constraint(operand, pltpu.HBM) for operand in operands])
    act, queue = pl.pallas_call(
        place,
        out_shape=shapes,
        in_specs=[anywhere] * 2,
        out_specs=(anywhere, anywhere),
        scratch_shapes=[
            pltpu.VMEM((images, cells, channels), f32),
            pltpu.SemaphoreType.DMA((ticks + depth,)),
        ],
        compiler_params=pltpu.CompilerParams(vmem_limit_bytes=4 << 20),
        name="place",
    )(*made)
    return (
        act.reshape(1, ticks, images, height, width, channels),
        queue.reshape(1, depth, images, height, width, channels),
    )


def solution(mesh):
    return jax.shard_map(
        per_device,
        mesh=mesh,
        in_specs=(
            P("segment", "dp", None, None, None),
            P(None, "dp", None, None, None),
            P("segment", None, "dp", None, None, None),
            P("segment", None, None, None),
            P("segment", None, None),
            P("segment", None, None),
        ),
        out_specs=(
            P("segment", None, "dp", None, None, None),
            P("segment", None, "dp", None, None, None),
        ),
        check_vma=False,
    )
```

```python
import functools

import jax
import jax.numpy as jnp
from jax import lax
from jax.experimental import pallas as pl
from jax.experimental.pallas import tpu as pltpu
from jax.sharding import PartitionSpec as P

MESH = pl.DeviceIdType.MESH
EPS = 1e-05
SIDE = 8
LANES = 128
PAIR = 2
SECTIONS = 8
PARTS = 1
AHEAD = 0
DIRECT = 2
BY_ZERO = 14
LATE = 1


def merge_four(mean, spread, step):
    lane = lax.broadcasted_iota(jnp.int32, mean.shape, 1)
    digit = (lane // step) % 4

    def around(v):
        others = []
        for k in range(1, 4):
            ahead = pltpu.roll(v, LANES - k * step, 1)
            behind = pltpu.roll(v, (4 - k) * step, 1)
            others.append(jnp.where(digit < 4 - k, ahead, behind))
        return [v] + others

    means = around(mean)
    spreads = around(spread)
    mean = 0.25 * ((means[0] + means[1]) + (means[2] + means[3]))
    between = [jnp.square(m - mean) for m in means]
    spread = 0.25 * (
        ((spreads[0] + between[0]) + (spreads[1] + between[1]))
        + ((spreads[2] + between[2]) + (spreads[3] + between[3]))
    )
    return mean, spread


def fill_patches(x, gain, shift, patches):
    images, cells, channels = x.shape
    column = lax.broadcasted_iota(jnp.int32, (cells, LANES), 0) % SIDE
    edge = jnp.zeros((SIDE, LANES), jnp.float32)
    for lo in range(0, channels, LANES):
        part = x[:, :, lo : lo + LANES]
        mean = jnp.mean(part, axis=1)
        spread = jnp.mean(jnp.square(part - mean[:, None]), axis=1)
        for step in (1, 4):
            mean, spread = merge_four(mean, spread, step)
        scale = lax.rsqrt(spread + EPS) * gain[:, lo : lo + LANES]
        for image in range(images):
            u = (part[image] - mean[image : image + 1]) * scale[image : image + 1] + shift[:, lo : lo + LANES]
            a = u / (1.0 + jnp.exp(-u))
            for c in range(3):
                if c == 0:
                    moved = jnp.where(column == 0, 0.0, pltpu.roll(a, 1, 0))
                elif c == 2:
                    moved = jnp.where(column == SIDE - 1, 0.0, pltpu.roll(a, cells - 1, 0))
                else:
                    moved = a
                for r in range(3):
                    if r == 0:
                        rows = jnp.concatenate([edge, moved[:-SIDE]], axis=0)
                    elif r == 2:
                        rows = jnp.concatenate([moved[SIDE:], edge], axis=0)
                    else:
                        rows = moved
                    at = (3 * r + c) * channels + lo
                    patches[image * cells : (image + 1) * cells, at : at + LANES] = rows.astype(jnp.bfloat16)


def window(
    images,
    ticks,
    handoff,
    fresh,
    skips,
    weights,
    gains,
    shifts,
    act,
    queue,
    w,
    gain,
    shift,
    bank,
    out_v,
    patches,
    load_sem,
    hand_send,
    hand_recv,
    mir_send,
    mir_recv,
    rel_send,
    out_sem,
):
    s = lax.axis_index("segment")
    steps = images * ticks
    handed = images * (ticks - 1)
    pairs = steps // PAIR
    half = SECTIONS // 2
    encoder = s < half
    cells, channels = bank.shape[1:]
    side = steps
    spare = 2 * steps

    load_x = pltpu.make_async_copy(handoff, bank.at[pl.ds(0, images)], load_sem.at[0])
    load_w = [pltpu.make_async_copy(weights.at[k], w.at[k], load_sem.at[1 + k]) for k in range(2)]
    load_fresh = pltpu.make_async_copy(fresh, bank.at[pl.ds(images, handed)], load_sem.at[3])
    keep_q = pltpu.make_async_copy(
        skips.at[pl.ds(steps, 2 * images)], queue.at[pl.ds(0, 2 * images)], load_sem.at[5]
    )
    load_gain = pltpu.make_async_copy(gains, gain, load_sem.at[6])
    load_shift = pltpu.make_async_copy(shifts, shift, load_sem.at[7])

    def load_q(count):
        return pltpu.make_async_copy(
            skips.at[pl.ds(0, count)], bank.at[pl.ds(side, count)], load_sem.at[4]
        )

    own_skips = ((s == half, images), (s == half + 1, 3 * images), (s >= half + 2, steps))
    load_gain.start()
    load_shift.start()
    load_x.start()
    for here, count in own_skips:
        pl.when(here)(load_q(count).start)

    @pl.when(encoder)
    def _():
        load_w[0].start()
        load_w[1].start()

    @pl.when(jnp.logical_not(encoder))
    def _():
        load_w[1].start()
        load_w[0].start()

    pl.when(s == 0)(load_fresh.start)
    pl.when(s == SECTIONS - 1)(keep_q.start)

    barrier = pltpu.get_barrier_semaphore()
    for k in range(1, SECTIONS):
        pl.semaphore_signal(barrier, 1, device_id={"segment": lax.rem(s + k, SECTIONS)}, device_id_type=MESH)

    def piece(h):
        return pl.ds(h * (cells // PARTS), cells // PARTS)

    def to_bank(source, slot, send, recv, target, h):
        return pltpu.make_async_remote_copy(
            source.at[piece(h)],
            bank.at[slot, piece(h)],
            send,
            recv,
            device_id={"segment": target},
            device_id_type=MESH,
        )

    def to_queue(source, slot, send, recv, target, h):
        return pltpu.make_async_remote_copy(
            source.at[piece(h)],
            queue.at[slot, piece(h)],
            send,
            recv,
            device_id={"segment": target},
            device_id_type=MESH,
        )

    def hand(n, h):
        return to_bank(
            out_v.at[n],
            n + images,
            hand_send.at[n, h],
            hand_recv.at[n + images, h],
            jnp.minimum(s + 1, SECTIONS - 1),
            h,
        )

    def arrived(recv):
        to_bank(out_v.at[0], spare, hand_send.at[0, 0], recv, jnp.int32(0), 0).wait_recv()

    def to_five(source, n, send, h):
        @pl.when(n < 2 * images)
        def _():
            to_bank(source, side + 3 * images + n, send, mir_recv.at[n, h], jnp.int32(5), h).start()

        @pl.when(n >= 2 * images)
        def _():
            to_queue(source, n - 2 * images, send, mir_recv.at[n, h], jnp.int32(5), h).start()

    def wait_x(p):
        @pl.when((s == 0) & (p == images // PAIR))
        def _():
            load_fresh.wait()

        for k in range(PAIR):
            n = p * PAIR + k
            for h in range(PARTS):

                @pl.when((s > 0) & (n >= images))
                def _():
                    arrived(hand_recv.at[n, h])

                @pl.when((s == 2) & (n >= images + AHEAD))
                def _():
                    m = n - images
                    to_queue(bank.at[n], m, rel_send.at[m, h], mir_recv.at[m, h], jnp.int32(6), h).start()

    def convolve(slot, kind):
        g = jnp.where(kind == 0, gain[0:1], gain[1:2])
        b = jnp.where(kind == 0, shift[0:1], shift[1:2])
        fill_patches(bank[pl.ds(slot, PAIR)], g, b, patches)
        return jnp.dot(patches[...], w[kind], preferred_element_type=jnp.float32).reshape(PAIR, cells, channels)

    def step(p, start):
        early = encoder | ((s == half) & (p * PAIR >= images))
        if not start:
            pl.when(early)(lambda: wait_x(p))

        @pl.when((s == half + 1) & (p * PAIR >= 3 * images))
        def _():
            for k in range(PAIR):
                for h in range(PARTS):
                    arrived(mir_recv.at[p * PAIR + k - 3 * images, h])

        if start:
            load_gain.wait()
            load_shift.wait()
            load_x.wait()
            for here, count in own_skips:
                pl.when(here)(load_q(count).wait)
            pl.when(encoder)(load_w[0].wait)
            pl.when(jnp.logical_not(encoder))(load_w[1].wait)
        n = p * PAIR
        kind = jnp.where(encoder, 0, 1)
        first = convolve(jnp.where(early, n, side + n), kind)
        bank[pl.ds(spare, PAIR)] = first
        if start:
            pl.when(encoder)(load_w[1].wait)
            pl.when(jnp.logical_not(encoder))(load_w[0].wait)
        else:
            pl.when(jnp.logical_not(early))(lambda: wait_x(p))
        second = convolve(jnp.where(encoder, spare, n), 1 - kind)
        total = bank[pl.ds(n, PAIR)] + second
        out_v[pl.ds(n, PAIR)] = jnp.where(encoder, total, total + bank[pl.ds(spare, PAIR)])
        if start:
            pl.semaphore_wait(barrier, SECTIONS - 1)
        for k in range(PAIR):
            send(p * PAIR + k)
        if not start:
            for k in range(PAIR):
                relay((p - 1) * PAIR + k)

    def send(n):
        for h in range(PARTS):
            pl.when((s < SECTIONS - 1) & (n < handed))(lambda h=h: hand(n, h).start())

        for h in range(PARTS):

            @pl.when(s == 0)
            def _():
                to_queue(
                    out_v.at[n], n + 2 * images, mir_send.at[n, h], mir_recv.at[n, h], jnp.int32(7), h
                ).start()

            @pl.when((s == 1) & ((n < AHEAD) | (n >= handed)))
            def _():
                to_queue(out_v.at[n], n, mir_send.at[n, h], mir_recv.at[n, h], jnp.int32(6), h).start()

            @pl.when((s == 2) & (n >= DIRECT) & (n < handed + LATE))
            def _():
                to_bank(out_v.at[n], side + n, mir_send.at[n, h], mir_recv.at[n, h], jnp.int32(1), h).start()

            @pl.when((s == 2) & ((n < DIRECT) | (n >= handed + LATE)))
            def _():
                to_five(out_v.at[n], n, mir_send.at[n, h], h)

            @pl.when((s == 3) & (n >= handed))
            def _():
                to_queue(out_v.at[n], n - handed, mir_send.at[n, h], mir_recv.at[n, h], jnp.int32(4), h).start()

        pltpu.make_async_copy(out_v.at[n], act.at[n], out_sem.at[n]).start()

    def relay(m):
        for h in range(PARTS):

            @pl.when((s == 1) & (m >= DIRECT) & (m < handed + LATE))
            def _():
                arrived(mir_recv.at[m, h])

                @pl.when(m == BY_ZERO)
                def _():
                    to_bank(
                        bank.at[side + m], side + m, rel_send.at[m, h], mir_recv.at[m, h], jnp.int32(0), h
                    ).start()

                @pl.when(m != BY_ZERO)
                def _():
                    to_five(bank.at[side + m], m, rel_send.at[m, h], h)

    step(jnp.int32(0), True)
    lax.fori_loop(1, pairs, lambda p, carry: (step(p, False), carry)[1], 0)

    @pl.when(s == 0)
    def _():
        for h in range(PARTS):
            arrived(mir_recv.at[BY_ZERO, h])
            to_five(bank.at[side + BY_ZERO], jnp.int32(BY_ZERO), rel_send.at[BY_ZERO, h], h)

    def drain(n, carry):
        for h in range(PARTS):
            pl.when((s < SECTIONS - 1) & (n < handed))(lambda h=h: hand(n, h).wait_send())

            @pl.when((s == 0) | (s == 2) | ((s == 1) & (n < AHEAD)) | (((s == 1) | (s == 3)) & (n >= handed)))
            def _():
                to_bank(out_v.at[n], spare, mir_send.at[n, h], mir_recv.at[n, h], jnp.int32(7), h).wait_send()

            @pl.when(
                ((s == 0) & (n == BY_ZERO))
                | ((s == 1) & (n >= DIRECT) & (n < handed + LATE))
                | ((s == 2) & (n >= AHEAD) & (n < handed))
            )
            def _():
                to_bank(out_v.at[n], spare, rel_send.at[n, h], mir_recv.at[n, h], jnp.int32(6), h).wait_send()

            @pl.when(((s == 4) & (n >= handed)) | ((s == 5) & (n >= 2 * images)) | (s >= 6))
            def _():
                arrived(mir_recv.at[n, h])

        pltpu.make_async_copy(out_v.at[n], act.at[n], out_sem.at[n]).wait()
        return carry

    lax.fori_loop(0, steps, drain, 0)
    pl.when(s == SECTIONS - 1)(keep_q.wait)


def place(act, queue, act_out, queue_out, zeros, sem):
    s = lax.axis_index("segment")
    depth = jnp.where(s < SECTIONS // 2, 0, 2 * s - SECTIONS + 1)
    images = zeros.shape[0]
    slots = queue.shape[0] // images
    ticks = act.shape[0] // images
    for t in range(ticks):
        rows = pl.ds(t * images, images)
        pltpu.make_async_copy(act.at[rows], act_out.at[rows], sem.at[t]).start()
    for k in range(slots):
        rows = pl.ds(k * images, images)
        pl.when(k < depth)(pltpu.make_async_copy(queue.at[rows], queue_out.at[rows], sem.at[ticks + k]).start)
    zeros[...] = jnp.zeros_like(zeros)
    for k in range(slots):
        rows = pl.ds(k * images, images)
        pl.when(k >= depth)(pltpu.make_async_copy(zeros, queue_out.at[rows], sem.at[ticks + k]).start)
    for t in range(ticks):
        rows = pl.ds(t * images, images)
        pltpu.make_async_copy(act.at[rows], act_out.at[rows], sem.at[t]).wait()
    for k in range(slots):
        rows = pl.ds(k * images, images)
        pltpu.make_async_copy(zeros, queue_out.at[rows], sem.at[ticks + k]).wait()


def per_device(handoff, fresh, skip_queue, conv_weight, norm_gain, norm_shift):
    _, images, height, width, channels = handoff.shape
    ticks = fresh.shape[0] + 1
    depth = skip_queue.shape[1]
    steps = images * ticks
    cells = height * width
    f32 = jnp.float32
    anywhere = pl.BlockSpec(memory_space=pl.ANY)
    shapes = (
        jax.ShapeDtypeStruct((steps, cells, channels), f32),
        jax.ShapeDtypeStruct((images * depth, cells, channels), f32),
    )
    operands = (
        handoff.reshape(images, cells, channels),
        fresh.reshape(steps - images, cells, channels),
        skip_queue.reshape(images * depth, cells, channels),
        conv_weight[0],
        norm_gain[0],
        norm_shift[0],
    )
    made = pl.pallas_call(
        functools.partial(window, images, ticks),
        out_shape=shapes,
        in_specs=[anywhere] * 6,
        out_specs=(anywhere, anywhere),
        scratch_shapes=[
            pltpu.VMEM((2, 9 * channels, channels), jnp.bfloat16),
            pltpu.VMEM((2, channels), f32),
            pltpu.VMEM((2, channels), f32),
            pltpu.VMEM((2 * steps + PAIR, cells, channels), f32),
            pltpu.VMEM((steps, cells, channels), f32),
            pltpu.VMEM((PAIR * cells, 9 * channels), jnp.bfloat16),
            pltpu.SemaphoreType.DMA((8,)),
            pltpu.SemaphoreType.DMA((steps, PARTS)),
            pltpu.SemaphoreType.DMA((steps, PARTS)),
            pltpu.SemaphoreType.DMA((steps, PARTS)),
            pltpu.SemaphoreType.DMA((steps, PARTS)),
            pltpu.SemaphoreType.DMA((steps, PARTS)),
            pltpu.SemaphoreType.DMA((steps,)),
        ],
        compiler_params=pltpu.CompilerParams(
            collective_id=0, has_side_effects=True, vmem_limit_bytes=36 << 20
        ),
        cost_estimate=pl.CostEstimate(
            flops=4 * steps * cells * 9 * channels * channels, bytes_accessed=20 << 20, transcendentals=0
        ),
        name="window",
    )(*[pltpu.with_memory_space_constraint(operand, pltpu.HBM) for operand in operands])
    act, queue = pl.pallas_call(
        place,
        out_shape=shapes,
        in_specs=[anywhere] * 2,
        out_specs=(anywhere, anywhere),
        scratch_shapes=[
            pltpu.VMEM((images, cells, channels), f32),
            pltpu.SemaphoreType.DMA((ticks + depth,)),
        ],
        compiler_params=pltpu.CompilerParams(vmem_limit_bytes=4 << 20),
        name="place",
    )(*made)
    return (
        act.reshape(1, ticks, images, height, width, channels),
        queue.reshape(1, depth, images, height, width, channels),
    )


def solution(mesh):
    return jax.shard_map(
        per_device,
        mesh=mesh,
        in_specs=(
            P("segment", "dp", None, None, None),
            P(None, "dp", None, None, None),
            P("segment", None, "dp", None, None, None),
            P("segment", None, None, None),
            P("segment", None, None),
            P("segment", None, None),
        ),
        out_specs=(
            P("segment", None, "dp", None, None, None),
            P("segment", None, "dp", None, None, None),
        ),
        check_vma=False,
    )
```

```python
import functools

import jax
import jax.numpy as jnp
from jax import lax
from jax.experimental import pallas as pl
from jax.experimental.pallas import tpu as pltpu
from jax.sharding import PartitionSpec as P

MESH = pl.DeviceIdType.MESH
EPS = 1e-05
SIDE = 8
LANES = 128
PAIR = 2
SECTIONS = 8
PARTS = 1
AHEAD = 0
DIRECT = 1
BY_ZERO = 14
CUT = 24
HELD = 2


def merge_four(mean, spread, step):
    lane = lax.broadcasted_iota(jnp.int32, mean.shape, 1)
    digit = (lane // step) % 4

    def around(v):
        others = []
        for k in range(1, 4):
            ahead = pltpu.roll(v, LANES - k * step, 1)
            behind = pltpu.roll(v, (4 - k) * step, 1)
            others.append(jnp.where(digit < 4 - k, ahead, behind))
        return [v] + others

    means = around(mean)
    spreads = around(spread)
    mean = 0.25 * ((means[0] + means[1]) + (means[2] + means[3]))
    between = [jnp.square(m - mean) for m in means]
    spread = 0.25 * (
        ((spreads[0] + between[0]) + (spreads[1] + between[1]))
        + ((spreads[2] + between[2]) + (spreads[3] + between[3]))
    )
    return mean, spread


def fill_patches(x, gain, shift, patches):
    images, cells, channels = x.shape
    column = lax.broadcasted_iota(jnp.int32, (cells, LANES), 0) % SIDE
    edge = jnp.zeros((SIDE, LANES), jnp.float32)
    for lo in range(0, channels, LANES):
        part = x[:, :, lo : lo + LANES]
        mean = jnp.mean(part, axis=1)
        spread = jnp.mean(jnp.square(part - mean[:, None]), axis=1)
        for step in (1, 4):
            mean, spread = merge_four(mean, spread, step)
        scale = lax.rsqrt(spread + EPS) * gain[:, lo : lo + LANES]
        for image in range(images):
            u = (part[image] - mean[image : image + 1]) * scale[image : image + 1] + shift[:, lo : lo + LANES]
            a = u / (1.0 + jnp.exp(-u))
            for c in range(3):
                if c == 0:
                    moved = jnp.where(column == 0, 0.0, pltpu.roll(a, 1, 0))
                elif c == 2:
                    moved = jnp.where(column == SIDE - 1, 0.0, pltpu.roll(a, cells - 1, 0))
                else:
                    moved = a
                for r in range(3):
                    if r == 0:
                        rows = jnp.concatenate([edge, moved[:-SIDE]], axis=0)
                    elif r == 2:
                        rows = jnp.concatenate([moved[SIDE:], edge], axis=0)
                    else:
                        rows = moved
                    at = (3 * r + c) * channels + lo
                    patches[image * cells : (image + 1) * cells, at : at + LANES] = rows.astype(jnp.bfloat16)


def window(
    images,
    ticks,
    handoff,
    fresh,
    skips,
    weights,
    gains,
    shifts,
    act,
    queue,
    w,
    gain,
    shift,
    bank,
    out_v,
    patches,
    load_sem,
    hand_send,
    hand_recv,
    mir_send,
    mir_recv,
    rel_send,
    out_sem,
):
    s = lax.axis_index("segment")
    steps = images * ticks
    handed = images * (ticks - 1)
    pairs = steps // PAIR
    half = SECTIONS // 2
    encoder = s < half
    cells, channels = bank.shape[1:]
    side = steps
    spare = 2 * steps

    load_x = pltpu.make_async_copy(handoff, bank.at[pl.ds(0, images)], load_sem.at[0])
    load_w = [pltpu.make_async_copy(weights.at[k], w.at[k], load_sem.at[1 + k]) for k in range(2)]
    load_fresh = pltpu.make_async_copy(fresh, bank.at[pl.ds(images, handed)], load_sem.at[3])
    keep_q = pltpu.make_async_copy(
        skips.at[pl.ds(steps, 2 * images)], queue.at[pl.ds(0, 2 * images)], load_sem.at[5]
    )
    load_gain = pltpu.make_async_copy(gains, gain, load_sem.at[6])
    load_shift = pltpu.make_async_copy(shifts, shift, load_sem.at[7])

    def load_q(count):
        return pltpu.make_async_copy(
            skips.at[pl.ds(0, count)], bank.at[pl.ds(side, count)], load_sem.at[4]
        )

    own_skips = ((s == half, images), (s == half + 1, 3 * images), (s >= half + 2, steps))
    load_gain.start()
    load_shift.start()
    load_x.start()
    for here, count in own_skips:
        pl.when(here)(load_q(count).start)

    @pl.when(encoder)
    def _():
        load_w[0].start()
        load_w[1].start()

    @pl.when(jnp.logical_not(encoder))
    def _():
        load_w[1].start()
        load_w[0].start()

    pl.when(s == 0)(load_fresh.start)
    pl.when(s == SECTIONS - 1)(keep_q.start)

    barrier = pltpu.get_barrier_semaphore()
    for k in range(1, SECTIONS):
        pl.semaphore_signal(barrier, 1, device_id={"segment": lax.rem(s + k, SECTIONS)}, device_id_type=MESH)

    def piece(h):
        return pl.ds(h * (cells // PARTS), cells // PARTS)

    def to_bank(source, slot, send, recv, target, h):
        return pltpu.make_async_remote_copy(
            source.at[piece(h)],
            bank.at[slot, piece(h)],
            send,
            recv,
            device_id={"segment": target},
            device_id_type=MESH,
        )

    def to_queue(source, slot, send, recv, target, h):
        return pltpu.make_async_remote_copy(
            source.at[piece(h)],
            queue.at[slot, piece(h)],
            send,
            recv,
            device_id={"segment": target},
            device_id_type=MESH,
        )

    def hand(n, h):
        return to_bank(
            out_v.at[n],
            n + images,
            hand_send.at[n, h],
            hand_recv.at[n + images, h],
            jnp.minimum(s + 1, SECTIONS - 1),
            h,
        )

    def arrived(recv):
        to_bank(out_v.at[0], spare, hand_send.at[0, 0], recv, jnp.int32(0), 0).wait_recv()

    def to_five(source, n, send, h):
        @pl.when(n < 2 * images)
        def _():
            to_bank(source, side + 3 * images + n, send, mir_recv.at[n, h], jnp.int32(5), h).start()

        @pl.when(n >= 2 * images)
        def _():
            to_queue(source, n - 2 * images, send, mir_recv.at[n, h], jnp.int32(5), h).start()

    def split_to_five(source, slot, send, rows):
        return pltpu.make_async_remote_copy(
            source.at[slot, rows],
            queue.at[handed - 2 * images, rows],
            send.at[handed, 0],
            mir_recv.at[handed, 0],
            device_id={"segment": jnp.int32(5)},
            device_id_type=MESH,
        )

    def wait_x(p):
        @pl.when((s == 0) & (p == images // PAIR))
        def _():
            load_fresh.wait()

        for k in range(PAIR):
            n = p * PAIR + k
            for h in range(PARTS):

                @pl.when((s > 0) & (n >= images))
                def _():
                    arrived(hand_recv.at[n, h])

                @pl.when((s == 2) & (n >= images + AHEAD))
                def _():
                    m = n - images
                    to_queue(bank.at[n], m, rel_send.at[m, h], mir_recv.at[m, h], jnp.int32(6), h).start()

    def convolve(slot, kind):
        g = jnp.where(kind == 0, gain[0:1], gain[1:2])
        b = jnp.where(kind == 0, shift[0:1], shift[1:2])
        fill_patches(bank[pl.ds(slot, PAIR)], g, b, patches)
        return jnp.dot(patches[...], w[kind], preferred_element_type=jnp.float32).reshape(PAIR, cells, channels)

    def step(p, start):
        early = encoder | ((s == half) & (p * PAIR >= images))
        if not start:
            pl.when(early)(lambda: wait_x(p))

        @pl.when((s == half + 1) & (p * PAIR >= 3 * images))
        def _():
            for k in range(PAIR):
                for h in range(PARTS):
                    arrived(mir_recv.at[p * PAIR + k - 3 * images, h])

        if start:
            load_gain.wait()
            load_shift.wait()
            load_x.wait()
            for here, count in own_skips:
                pl.when(here)(load_q(count).wait)
            pl.when(encoder)(load_w[0].wait)
            pl.when(jnp.logical_not(encoder))(load_w[1].wait)
        n = p * PAIR
        kind = jnp.where(encoder, 0, 1)
        first = convolve(jnp.where(early, n, side + n), kind)
        bank[pl.ds(spare, PAIR)] = first
        if start:
            pl.when(encoder)(load_w[1].wait)
            pl.when(jnp.logical_not(encoder))(load_w[0].wait)
        else:
            pl.when(jnp.logical_not(early))(lambda: wait_x(p))
        second = convolve(jnp.where(encoder, spare, n), 1 - kind)
        total = bank[pl.ds(n, PAIR)] + second
        out_v[pl.ds(n, PAIR)] = jnp.where(encoder, total, total + bank[pl.ds(spare, PAIR)])
        if start:
            pl.semaphore_wait(barrier, SECTIONS - 1)
        for k in range(PAIR):
            send(p * PAIR + k)
        if not start:
            for k in range(PAIR):
                relay((p - 1) * PAIR + k)

    def send(n):
        for h in range(PARTS):
            pl.when((s < SECTIONS - 1) & (n < handed))(lambda h=h: hand(n, h).start())

        for h in range(PARTS):

            @pl.when((s == 0) & (n < steps - HELD))
            def _():
                to_queue(
                    out_v.at[n], n + 2 * images, mir_send.at[n, h], mir_recv.at[n, h], jnp.int32(7), h
                ).start()

            @pl.when((s == 1) & ((n < AHEAD) | (n >= handed)))
            def _():
                to_queue(out_v.at[n], n, mir_send.at[n, h], mir_recv.at[n, h], jnp.int32(6), h).start()

            @pl.when((s == 2) & (n >= DIRECT) & (n < handed))
            def _():
                to_bank(out_v.at[n], side + n, mir_send.at[n, h], mir_recv.at[n, h], jnp.int32(1), h).start()

            @pl.when((s == 2) & ((n < DIRECT) | (n > handed)))
            def _():
                to_five(out_v.at[n], n, mir_send.at[n, h], h)

            @pl.when((s == 3) & (n >= handed))
            def _():
                to_queue(out_v.at[n], n - handed, mir_send.at[n, h], mir_recv.at[n, h], jnp.int32(4), h).start()

        @pl.when((s == 2) & (n == handed))
        def _():
            split_to_five(out_v, handed, mir_send, slice(0, CUT)).start()
            pltpu.make_async_remote_copy(
                out_v.at[handed, CUT:],
                bank.at[side + handed, CUT:],
                mir_send.at[handed, 0],
                mir_recv.at[handed, 0],
                device_id={"segment": jnp.int32(1)},
                device_id_type=MESH,
            ).start()

        pltpu.make_async_copy(out_v.at[n], act.at[n], out_sem.at[n]).start()

    def relay(m):
        for h in range(PARTS):

            @pl.when((s == 1) & (m >= DIRECT) & (m < handed))
            def _():
                arrived(mir_recv.at[m, h])

                @pl.when(m == BY_ZERO)
                def _():
                    to_bank(
                        bank.at[side + m], side + m, rel_send.at[m, h], mir_recv.at[m, h], jnp.int32(0), h
                    ).start()

                @pl.when(m != BY_ZERO)
                def _():
                    to_five(bank.at[side + m], m, rel_send.at[m, h], h)

        @pl.when((s == 1) & (m == handed))
        def _():
            late = split_to_five(bank, side + handed, rel_send, slice(CUT, None))
            late.wait_recv()
            late.start()

    step(jnp.int32(0), True)
    lax.fori_loop(1, pairs, lambda p, carry: (step(p, False), carry)[1], 0)

    @pl.when(s == 0)
    def _():
        for h in range(PARTS):
            arrived(mir_recv.at[BY_ZERO, h])
            to_five(bank.at[side + BY_ZERO], jnp.int32(BY_ZERO), rel_send.at[BY_ZERO, h], h)
        for n in range(steps - HELD, steps):
            for h in range(PARTS):
                to_queue(
                    out_v.at[n], n + 2 * images, mir_send.at[n, h], mir_recv.at[n, h], jnp.int32(7), h
                ).start()

    def drain(n, carry):
        for h in range(PARTS):
            pl.when((s < SECTIONS - 1) & (n < handed))(lambda h=h: hand(n, h).wait_send())

            @pl.when((s == 0) | (s == 2) | ((s == 1) & (n < AHEAD)) | (((s == 1) | (s == 3)) & (n >= handed)))
            def _():
                to_bank(out_v.at[n], spare, mir_send.at[n, h], mir_recv.at[n, h], jnp.int32(7), h).wait_send()

            @pl.when(
                ((s == 0) & (n == BY_ZERO))
                | ((s == 1) & (n >= DIRECT) & (n < handed))
                | ((s == 2) & (n >= AHEAD) & (n < handed))
            )
            def _():
                to_bank(out_v.at[n], spare, rel_send.at[n, h], mir_recv.at[n, h], jnp.int32(6), h).wait_send()

            @pl.when(((s == 4) & (n >= handed)) | ((s == 5) & (n >= 2 * images)) | (s >= 6))
            def _():
                arrived(mir_recv.at[n, h])

        pltpu.make_async_copy(out_v.at[n], act.at[n], out_sem.at[n]).wait()
        return carry

    lax.fori_loop(0, steps, drain, 0)
    pl.when(s == 1)(split_to_five(bank, side + handed, rel_send, slice(CUT, None)).wait_send)
    pl.when(s == SECTIONS - 1)(keep_q.wait)


def place(act, queue, act_out, queue_out, zeros, sem):
    s = lax.axis_index("segment")
    depth = jnp.where(s < SECTIONS // 2, 0, 2 * s - SECTIONS + 1)
    images = zeros.shape[0]
    slots = queue.shape[0] // images
    ticks = act.shape[0] // images
    for t in range(ticks):
        rows = pl.ds(t * images, images)
        pltpu.make_async_copy(act.at[rows], act_out.at[rows], sem.at[t]).start()
    for k in range(slots):
        rows = pl.ds(k * images, images)
        pl.when(k < depth)(pltpu.make_async_copy(queue.at[rows], queue_out.at[rows], sem.at[ticks + k]).start)
    zeros[...] = jnp.zeros_like(zeros)
    for k in range(slots):
        rows = pl.ds(k * images, images)
        pl.when(k >= depth)(pltpu.make_async_copy(zeros, queue_out.at[rows], sem.at[ticks + k]).start)
    for t in range(ticks):
        rows = pl.ds(t * images, images)
        pltpu.make_async_copy(act.at[rows], act_out.at[rows], sem.at[t]).wait()
    for k in range(slots):
        rows = pl.ds(k * images, images)
        pltpu.make_async_copy(zeros, queue_out.at[rows], sem.at[ticks + k]).wait()


def per_device(handoff, fresh, skip_queue, conv_weight, norm_gain, norm_shift):
    _, images, height, width, channels = handoff.shape
    ticks = fresh.shape[0] + 1
    depth = skip_queue.shape[1]
    steps = images * ticks
    cells = height * width
    f32 = jnp.float32
    anywhere = pl.BlockSpec(memory_space=pl.ANY)
    shapes = (
        jax.ShapeDtypeStruct((steps, cells, channels), f32),
        jax.ShapeDtypeStruct((images * depth, cells, channels), f32),
    )
    operands = (
        handoff.reshape(images, cells, channels),
        fresh.reshape(steps - images, cells, channels),
        skip_queue.reshape(images * depth, cells, channels),
        conv_weight[0],
        norm_gain[0],
        norm_shift[0],
    )
    made = pl.pallas_call(
        functools.partial(window, images, ticks),
        out_shape=shapes,
        in_specs=[anywhere] * 6,
        out_specs=(anywhere, anywhere),
        scratch_shapes=[
            pltpu.VMEM((2, 9 * channels, channels), jnp.bfloat16),
            pltpu.VMEM((2, channels), f32),
            pltpu.VMEM((2, channels), f32),
            pltpu.VMEM((2 * steps + PAIR, cells, channels), f32),
            pltpu.VMEM((steps, cells, channels), f32),
            pltpu.VMEM((PAIR * cells, 9 * channels), jnp.bfloat16),
            pltpu.SemaphoreType.DMA((8,)),
            pltpu.SemaphoreType.DMA((steps, PARTS)),
            pltpu.SemaphoreType.DMA((steps, PARTS)),
            pltpu.SemaphoreType.DMA((steps, PARTS)),
            pltpu.SemaphoreType.DMA((steps, PARTS)),
            pltpu.SemaphoreType.DMA((steps, PARTS)),
            pltpu.SemaphoreType.DMA((steps,)),
        ],
        compiler_params=pltpu.CompilerParams(
            collective_id=0, has_side_effects=True, vmem_limit_bytes=36 << 20
        ),
        cost_estimate=pl.CostEstimate(
            flops=4 * steps * cells * 9 * channels * channels, bytes_accessed=20 << 20, transcendentals=0
        ),
        name="window",
    )(*[pltpu.with_memory_space_constraint(operand, pltpu.HBM) for operand in operands])
    act, queue = pl.pallas_call(
        place,
        out_shape=shapes,
        in_specs=[anywhere] * 2,
        out_specs=(anywhere, anywhere),
        scratch_shapes=[
            pltpu.VMEM((images, cells, channels), f32),
            pltpu.SemaphoreType.DMA((ticks + depth,)),
        ],
        compiler_params=pltpu.CompilerParams(vmem_limit_bytes=4 << 20),
        name="place",
    )(*made)
    return (
        act.reshape(1, ticks, images, height, width, channels),
        queue.reshape(1, depth, images, height, width, channels),
    )


def solution(mesh):
    return jax.shard_map(
        per_device,
        mesh=mesh,
        in_specs=(
            P("segment", "dp", None, None, None),
            P(None, "dp", None, None, None),
            P("segment", None, "dp", None, None, None),
            P("segment", None, None, None),
            P("segment", None, None),
            P("segment", None, None),
        ),
        out_specs=(
            P("segment", None, "dp", None, None, None),
            P("segment", None, "dp", None, None, None),
        ),
        check_vma=False,
    )
```

```python
import functools

import jax
import jax.numpy as jnp
from jax import lax
from jax.experimental import pallas as pl
from jax.experimental.pallas import tpu as pltpu
from jax.sharding import PartitionSpec as P

MESH = pl.DeviceIdType.MESH
EPS = 1e-05
SIDE = 8
LANES = 128
PAIR = 2
SECTIONS = 8
PARTS = 1
AHEAD = 0
DIRECT = 1
BY_ZERO = 14
CUT = 24
HELD = 2


def merge_four(mean, spread, step):
    lane = lax.broadcasted_iota(jnp.int32, mean.shape, 1)
    digit = (lane // step) % 4

    def around(v):
        others = []
        for k in range(1, 4):
            ahead = pltpu.roll(v, LANES - k * step, 1)
            behind = pltpu.roll(v, (4 - k) * step, 1)
            others.append(jnp.where(digit < 4 - k, ahead, behind))
        return [v] + others

    means = around(mean)
    spreads = around(spread)
    mean = 0.25 * ((means[0] + means[1]) + (means[2] + means[3]))
    between = [jnp.square(m - mean) for m in means]
    spread = 0.25 * (
        ((spreads[0] + between[0]) + (spreads[1] + between[1]))
        + ((spreads[2] + between[2]) + (spreads[3] + between[3]))
    )
    return mean, spread


def fill_patches(x, gain, shift, patches):
    images, cells, channels = x.shape
    column = lax.broadcasted_iota(jnp.int32, (cells, LANES), 0) % SIDE
    edge = jnp.zeros((SIDE, LANES), jnp.float32)
    for lo in range(0, channels, LANES):
        part = x[:, :, lo : lo + LANES]
        mean = jnp.mean(part, axis=1)
        spread = jnp.mean(jnp.square(part - mean[:, None]), axis=1)
        for step in (1, 4):
            mean, spread = merge_four(mean, spread, step)
        scale = lax.rsqrt(spread + EPS) * gain[:, lo : lo + LANES]
        for image in range(images):
            u = (part[image] - mean[image : image + 1]) * scale[image : image + 1] + shift[:, lo : lo + LANES]
            a = u / (1.0 + jnp.exp(-u))
            for c in range(3):
                if c == 0:
                    moved = jnp.where(column == 0, 0.0, pltpu.roll(a, 1, 0))
                elif c == 2:
                    moved = jnp.where(column == SIDE - 1, 0.0, pltpu.roll(a, cells - 1, 0))
                else:
                    moved = a
                for r in range(3):
                    if r == 0:
                        rows = jnp.concatenate([edge, moved[:-SIDE]], axis=0)
                    elif r == 2:
                        rows = jnp.concatenate([moved[SIDE:], edge], axis=0)
                    else:
                        rows = moved
                    at = (3 * r + c) * channels + lo
                    patches[image * cells : (image + 1) * cells, at : at + LANES] = rows.astype(jnp.bfloat16)


def window(
    images,
    ticks,
    handoff,
    fresh,
    skips,
    weights,
    gains,
    shifts,
    act,
    queue,
    w,
    gain,
    shift,
    bank,
    out_v,
    patches,
    load_sem,
    hand_send,
    hand_recv,
    mir_send,
    mir_recv,
    rel_send,
    out_sem,
):
    s = lax.axis_index("segment")
    steps = images * ticks
    handed = images * (ticks - 1)
    pairs = steps // PAIR
    half = SECTIONS // 2
    encoder = s < half
    cells, channels = bank.shape[1:]
    side = steps
    spare = 2 * steps

    load_x = pltpu.make_async_copy(handoff, bank.at[pl.ds(0, images)], load_sem.at[0])
    load_w = [pltpu.make_async_copy(weights.at[k], w.at[k], load_sem.at[1 + k]) for k in range(2)]
    load_fresh = pltpu.make_async_copy(fresh, bank.at[pl.ds(images, handed)], load_sem.at[3])
    keep_q = pltpu.make_async_copy(
        skips.at[pl.ds(steps, 2 * images)], queue.at[pl.ds(0, 2 * images)], load_sem.at[5]
    )
    load_gain = pltpu.make_async_copy(gains, gain, load_sem.at[6])
    load_shift = pltpu.make_async_copy(shifts, shift, load_sem.at[7])

    def load_q(count):
        return pltpu.make_async_copy(
            skips.at[pl.ds(0, count)], bank.at[pl.ds(side, count)], load_sem.at[4]
        )

    own_skips = ((s == half, images), (s == half + 1, 3 * images), (s >= half + 2, steps))
    load_gain.start()
    load_shift.start()
    load_x.start()
    for here, count in own_skips:
        pl.when(here)(load_q(count).start)

    @pl.when(encoder)
    def _():
        load_w[0].start()
        load_w[1].start()

    @pl.when(jnp.logical_not(encoder))
    def _():
        load_w[1].start()
        load_w[0].start()

    pl.when(s == 0)(load_fresh.start)
    pl.when(s == SECTIONS - 1)(keep_q.start)

    barrier = pltpu.get_barrier_semaphore()
    for k in range(1, SECTIONS):
        pl.semaphore_signal(barrier, 1, device_id={"segment": lax.rem(s + k, SECTIONS)}, device_id_type=MESH)

    def piece(h):
        return pl.ds(h * (cells // PARTS), cells // PARTS)

    def to_bank(source, slot, send, recv, target, h):
        return pltpu.make_async_remote_copy(
            source.at[piece(h)],
            bank.at[slot, piece(h)],
            send,
            recv,
            device_id={"segment": target},
            device_id_type=MESH,
        )

    def to_queue(source, slot, send, recv, target, h):
        return pltpu.make_async_remote_copy(
            source.at[piece(h)],
            queue.at[slot, piece(h)],
            send,
            recv,
            device_id={"segment": target},
            device_id_type=MESH,
        )

    def hand(n, h):
        return to_bank(
            out_v.at[n],
            n + images,
            hand_send.at[n, h],
            hand_recv.at[n + images, h],
            jnp.minimum(s + 1, SECTIONS - 1),
            h,
        )

    def arrived(recv):
        to_bank(out_v.at[0], spare, hand_send.at[0, 0], recv, jnp.int32(0), 0).wait_recv()

    def to_five(source, n, send, h):
        @pl.when(n < 2 * images)
        def _():
            to_bank(source, side + 3 * images + n, send, mir_recv.at[n, h], jnp.int32(5), h).start()

        @pl.when(n >= 2 * images)
        def _():
            to_queue(source, n - 2 * images, send, mir_recv.at[n, h], jnp.int32(5), h).start()

    def split_to_five(source, slot, send, rows):
        return pltpu.make_async_remote_copy(
            source.at[slot, rows],
            queue.at[handed - 2 * images, rows],
            send.at[handed, 0],
            mir_recv.at[handed, 0],
            device_id={"segment": jnp.int32(5)},
            device_id_type=MESH,
        )

    def wait_x(p):
        @pl.when((s == 0) & (p == images // PAIR))
        def _():
            load_fresh.wait()

        for k in range(PAIR):
            n = p * PAIR + k
            for h in range(PARTS):

                @pl.when((s > 0) & (n >= images))
                def _():
                    arrived(hand_recv.at[n, h])

                @pl.when((s == 2) & (n >= images + AHEAD))
                def _():
                    m = n - images
                    to_queue(bank.at[n], m, rel_send.at[m, h], mir_recv.at[m, h], jnp.int32(6), h).start()

    def convolve(slot, kind):
        g = jnp.where(kind == 0, gain[0:1], gain[1:2])
        b = jnp.where(kind == 0, shift[0:1], shift[1:2])
        fill_patches(bank[pl.ds(slot, PAIR)], g, b, patches)
        return jnp.dot(patches[...], w[kind], preferred_element_type=jnp.float32).reshape(PAIR, cells, channels)

    def step(p, start):
        early = encoder | ((s == half) & (p * PAIR >= images))
        if not start:
            pl.when(early)(lambda: wait_x(p))

        @pl.when((s == half + 1) & (p * PAIR >= 3 * images))
        def _():
            for k in range(PAIR):
                for h in range(PARTS):
                    arrived(mir_recv.at[p * PAIR + k - 3 * images, h])

        if start:
            load_gain.wait()
            load_shift.wait()
            load_x.wait()
            for here, count in own_skips:
                pl.when(here)(load_q(count).wait)
            pl.when(encoder)(load_w[0].wait)
            pl.when(jnp.logical_not(encoder))(load_w[1].wait)
        n = p * PAIR
        kind = jnp.where(encoder, 0, 1)
        first = convolve(jnp.where(early, n, side + n), kind)
        bank[pl.ds(spare, PAIR)] = first
        if start:
            pl.when(encoder)(load_w[1].wait)
            pl.when(jnp.logical_not(encoder))(load_w[0].wait)
        else:
            pl.when(jnp.logical_not(early))(lambda: wait_x(p))
        second = convolve(jnp.where(encoder, spare, n), 1 - kind)
        total = bank[pl.ds(n, PAIR)] + second
        out_v[pl.ds(n, PAIR)] = jnp.where(encoder, total, total + bank[pl.ds(spare, PAIR)])
        if start:
            pl.semaphore_wait(barrier, SECTIONS - 1)
        for k in range(PAIR):
            send(p * PAIR + k)
        keep(n).start()
        if not start:
            for k in range(PAIR):
                relay((p - 1) * PAIR + k)

    def keep(n):
        return pltpu.make_async_copy(out_v.at[pl.ds(n, PAIR)], act.at[pl.ds(n, PAIR)], out_sem.at[n])

    def send(n):
        for h in range(PARTS):
            pl.when((s < SECTIONS - 1) & (n < handed))(lambda h=h: hand(n, h).start())

        for h in range(PARTS):

            @pl.when((s == 0) & (n < steps - HELD))
            def _():
                to_queue(
                    out_v.at[n], n + 2 * images, mir_send.at[n, h], mir_recv.at[n, h], jnp.int32(7), h
                ).start()

            @pl.when((s == 1) & ((n < AHEAD) | (n >= handed)))
            def _():
                to_queue(out_v.at[n], n, mir_send.at[n, h], mir_recv.at[n, h], jnp.int32(6), h).start()

            @pl.when((s == 2) & (n >= DIRECT) & (n < handed))
            def _():
                to_bank(out_v.at[n], side + n, mir_send.at[n, h], mir_recv.at[n, h], jnp.int32(1), h).start()

            @pl.when((s == 2) & ((n < DIRECT) | (n > handed)))
            def _():
                to_five(out_v.at[n], n, mir_send.at[n, h], h)

            @pl.when((s == 3) & (n >= handed))
            def _():
                to_queue(out_v.at[n], n - handed, mir_send.at[n, h], mir_recv.at[n, h], jnp.int32(4), h).start()

        @pl.when((s == 2) & (n == handed))
        def _():
            split_to_five(out_v, handed, mir_send, slice(0, CUT)).start()
            pltpu.make_async_remote_copy(
                out_v.at[handed, CUT:],
                bank.at[side + handed, CUT:],
                mir_send.at[handed, 0],
                mir_recv.at[handed, 0],
                device_id={"segment": jnp.int32(1)},
                device_id_type=MESH,
            ).start()


    def relay(m):
        for h in range(PARTS):

            @pl.when((s == 1) & (m >= DIRECT) & (m < handed))
            def _():
                arrived(mir_recv.at[m, h])

                @pl.when(m == BY_ZERO)
                def _():
                    to_bank(
                        bank.at[side + m], side + m, rel_send.at[m, h], mir_recv.at[m, h], jnp.int32(0), h
                    ).start()

                @pl.when(m != BY_ZERO)
                def _():
                    to_five(bank.at[side + m], m, rel_send.at[m, h], h)

        @pl.when((s == 1) & (m == handed))
        def _():
            late = split_to_five(bank, side + handed, rel_send, slice(CUT, None))
            late.wait_recv()
            late.start()

    step(jnp.int32(0), True)
    lax.fori_loop(1, pairs, lambda p, carry: (step(p, False), carry)[1], 0)

    @pl.when(s == 0)
    def _():
        for h in range(PARTS):
            arrived(mir_recv.at[BY_ZERO, h])
            to_five(bank.at[side + BY_ZERO], jnp.int32(BY_ZERO), rel_send.at[BY_ZERO, h], h)
        for n in range(steps - HELD, steps):
            for h in range(PARTS):
                to_queue(
                    out_v.at[n], n + 2 * images, mir_send.at[n, h], mir_recv.at[n, h], jnp.int32(7), h
                ).start()

    def drain(n, carry):
        for h in range(PARTS):
            pl.when((s < SECTIONS - 1) & (n < handed))(lambda h=h: hand(n, h).wait_send())

            @pl.when((s == 0) | (s == 2) | ((s == 1) & (n < AHEAD)) | (((s == 1) | (s == 3)) & (n >= handed)))
            def _():
                to_bank(out_v.at[n], spare, mir_send.at[n, h], mir_recv.at[n, h], jnp.int32(7), h).wait_send()

            @pl.when(
                ((s == 0) & (n == BY_ZERO))
                | ((s == 1) & (n >= DIRECT) & (n < handed))
                | ((s == 2) & (n >= AHEAD) & (n < handed))
            )
            def _():
                to_bank(out_v.at[n], spare, rel_send.at[n, h], mir_recv.at[n, h], jnp.int32(6), h).wait_send()

            @pl.when(((s == 4) & (n >= handed)) | ((s == 5) & (n >= 2 * images)) | (s >= 6))
            def _():
                arrived(mir_recv.at[n, h])

        pl.when(lax.rem(n, PAIR) == 0)(keep(n).wait)
        return carry

    lax.fori_loop(0, steps, drain, 0)
    pl.when(s == 1)(split_to_five(bank, side + handed, rel_send, slice(CUT, None)).wait_send)
    pl.when(s == SECTIONS - 1)(keep_q.wait)


def place(act, queue, act_out, queue_out, zeros, sem):
    s = lax.axis_index("segment")
    depth = jnp.where(s < SECTIONS // 2, 0, 2 * s - SECTIONS + 1)
    images = zeros.shape[0]
    slots = queue.shape[0] // images
    ticks = act.shape[0] // images
    for t in range(ticks):
        rows = pl.ds(t * images, images)
        pltpu.make_async_copy(act.at[rows], act_out.at[rows], sem.at[t]).start()
    for k in range(slots):
        rows = pl.ds(k * images, images)
        pl.when(k < depth)(pltpu.make_async_copy(queue.at[rows], queue_out.at[rows], sem.at[ticks + k]).start)
    zeros[...] = jnp.zeros_like(zeros)
    for k in range(slots):
        rows = pl.ds(k * images, images)
        pl.when(k >= depth)(pltpu.make_async_copy(zeros, queue_out.at[rows], sem.at[ticks + k]).start)
    for t in range(ticks):
        rows = pl.ds(t * images, images)
        pltpu.make_async_copy(act.at[rows], act_out.at[rows], sem.at[t]).wait()
    for k in range(slots):
        rows = pl.ds(k * images, images)
        pltpu.make_async_copy(zeros, queue_out.at[rows], sem.at[ticks + k]).wait()


def per_device(handoff, fresh, skip_queue, conv_weight, norm_gain, norm_shift):
    _, images, height, width, channels = handoff.shape
    ticks = fresh.shape[0] + 1
    depth = skip_queue.shape[1]
    steps = images * ticks
    cells = height * width
    f32 = jnp.float32
    anywhere = pl.BlockSpec(memory_space=pl.ANY)
    shapes = (
        jax.ShapeDtypeStruct((steps, cells, channels), f32),
        jax.ShapeDtypeStruct((images * depth, cells, channels), f32),
    )
    operands = (
        handoff.reshape(images, cells, channels),
        fresh.reshape(steps - images, cells, channels),
        skip_queue.reshape(images * depth, cells, channels),
        conv_weight[0],
        norm_gain[0],
        norm_shift[0],
    )
    made = pl.pallas_call(
        functools.partial(window, images, ticks),
        out_shape=shapes,
        in_specs=[anywhere] * 6,
        out_specs=(anywhere, anywhere),
        scratch_shapes=[
            pltpu.VMEM((2, 9 * channels, channels), jnp.bfloat16),
            pltpu.VMEM((2, channels), f32),
            pltpu.VMEM((2, channels), f32),
            pltpu.VMEM((2 * steps + PAIR, cells, channels), f32),
            pltpu.VMEM((steps, cells, channels), f32),
            pltpu.VMEM((PAIR * cells, 9 * channels), jnp.bfloat16),
            pltpu.SemaphoreType.DMA((8,)),
            pltpu.SemaphoreType.DMA((steps, PARTS)),
            pltpu.SemaphoreType.DMA((steps, PARTS)),
            pltpu.SemaphoreType.DMA((steps, PARTS)),
            pltpu.SemaphoreType.DMA((steps, PARTS)),
            pltpu.SemaphoreType.DMA((steps, PARTS)),
            pltpu.SemaphoreType.DMA((steps,)),
        ],
        compiler_params=pltpu.CompilerParams(
            collective_id=0, has_side_effects=True, vmem_limit_bytes=36 << 20
        ),
        cost_estimate=pl.CostEstimate(
            flops=4 * steps * cells * 9 * channels * channels, bytes_accessed=20 << 20, transcendentals=0
        ),
        name="window",
    )(*[pltpu.with_memory_space_constraint(operand, pltpu.HBM) for operand in operands])
    act, queue = pl.pallas_call(
        place,
        out_shape=shapes,
        in_specs=[anywhere] * 2,
        out_specs=(anywhere, anywhere),
        scratch_shapes=[
            pltpu.VMEM((images, cells, channels), f32),
            pltpu.SemaphoreType.DMA((ticks + depth,)),
        ],
        compiler_params=pltpu.CompilerParams(vmem_limit_bytes=4 << 20),
        name="place",
    )(*made)
    return (
        act.reshape(1, ticks, images, height, width, channels),
        queue.reshape(1, depth, images, height, width, channels),
    )


def solution(mesh):
    return jax.shard_map(
        per_device,
        mesh=mesh,
        in_specs=(
            P("segment", "dp", None, None, None),
            P(None, "dp", None, None, None),
            P("segment", None, "dp", None, None, None),
            P("segment", None, None, None),
            P("segment", None, None),
            P("segment", None, None),
        ),
        out_specs=(
            P("segment", None, "dp", None, None, None),
            P("segment", None, "dp", None, None, None),
        ),
        check_vma=False,
    )
```
